32 devices in a mesh: row: 8 (over y, x, core), col: 4 (over z).
Axes of the slice: x: 2, y: 2, z: 4, core: 2. Of those that a mesh axis runs over, the one named last changes fastest.
Arguments:
- sources: bfloat16 [16, 8192], P(None, ('row', 'col')), may hold values from -6 to 6
- dipole_tiles: bfloat16 [1024, 256, 256], P(('row', 'col')), may hold values from -0.1875 to 0.1875
- dipole_rows: int32 [1024], P(('row', 'col')), may hold values from 0 to 3
- dipole_columns: int32 [1024], P(('row', 'col')), may hold values from 0 to 7
- dipole_count: int32 [32], P(('row', 'col')), may hold values from 1 to 32, as said below
- energies: float32 [8192], P(('row', 'col')), may hold values from -3 to 3
- h_tiles: bfloat16 [1024, 256, 256], P(('row', 'col')), may hold values from -0.0625 to 0.0625
- tile_rows: int32 [1024], P(('row', 'col')), may hold values from 0 to 3, as said below
- tile_columns: int32 [1024], P(('row', 'col')), may hold values from 0 to 7
- tile_count: int32 [32], P(('row', 'col')), may hold values from 1 to 32, as said below
Outputs:
- solution: float32 [64, 8192], P(None, ('row', 'col'))
- residual: float32 [64, 8192], P(None, ('row', 'col'))
- checksum: float32 [3, 64], replicated
The draws below stay inside these ranges and needn't reach their ends.
Inputs may be any that keep to these rules, and one draw needn't show every extreme that they name: `tile_rows`: for every Hamiltonian slot, padded ones too, the block row I does not exceed the block column J. `tile_count`: some device has all 32 slots live in every draw; the live slots of one device name distinct pairs of block row and block column. `dipole_count`: some device has all 32 slots live in every draw.
All inputs are finite; a program needn't handle non-finite values.
Results may differ from the reference program's by a relative error of at most 0.0003.
Values may be sent and summed in bfloat16 or wider, within the bound.
A program may use at most 128 MiB of HBM per device.

```python
import jax
import jax.numpy as jnp
from jax import lax

NV = 16
SHIFTS = 4
BLOCK = 256
KT = 32
KD = 32
ITERS = 3
ROW_BLOCKS = 4
COL_BLOCKS = 8
STATES = 8192


def tile_layout(key):
    devices = ROW_BLOCKS * COL_BLOCKS
    pairs = ROW_BLOCKS * COL_BLOCKS
    key = jax.random.fold_in(key, 11)
    key_score, key_count, key_full = jax.random.split(key, 3)
    device = jnp.arange(devices, dtype=jnp.int32)[:, None]
    pair = jnp.arange(pairs, dtype=jnp.int32)[None, :]
    upper = device // ROW_BLOCKS * ROW_BLOCKS + pair // COL_BLOCKS
    lower = pair % COL_BLOCKS * ROW_BLOCKS + device % ROW_BLOCKS
    valid = upper <= lower
    score = jax.random.randint(key_score, (devices, pairs), 0, 1 << 20, dtype=jnp.int32) * pairs + pair
    score = jnp.where(valid, score, -1 - pair)
    order = jnp.argsort(-score, axis=1, stable=True).astype(jnp.int32)
    usable = jnp.sum(valid.astype(jnp.int32), axis=1)
    slots = jnp.arange(KT, dtype=jnp.int32)[None, :] % usable[:, None]
    picked = jnp.take_along_axis(order, slots, axis=1)
    count = jax.random.randint(key_count, (devices,), max(1, KT // 4), KT + 1, dtype=jnp.int32)
    count = jnp.maximum(jnp.minimum(count, usable), 1)
    index = jnp.arange(devices, dtype=jnp.int32)
    full_score = jax.random.randint(key_full, (devices,), 0, 1 << 20, dtype=jnp.int32) * devices + index
    full_score = jnp.where(usable >= KT, full_score, -1 - index)
    full = jnp.argsort(-full_score, stable=True)[0].astype(jnp.int32)
    count = jnp.where(index == full, KT, count)
    return ((picked // COL_BLOCKS).reshape(-1), (picked % COL_BLOCKS).reshape(-1), count.astype(jnp.int32))


def dipole_layout(key):
    devices = ROW_BLOCKS * COL_BLOCKS
    key = jax.random.fold_in(key, 23)
    key_rows, key_columns, key_count, key_full = jax.random.split(key, 4)
    rows = jax.random.randint(key_rows, (devices * KD,), 0, ROW_BLOCKS, dtype=jnp.int32)
    columns = jax.random.randint(key_columns, (devices * KD,), 0, COL_BLOCKS, dtype=jnp.int32)
    count = jax.random.randint(key_count, (devices,), max(1, KD // 4), KD + 1, dtype=jnp.int32)
    full = jax.random.randint(key_full, (), 0, devices, dtype=jnp.int32)
    count = jnp.where(jnp.arange(devices, dtype=jnp.int32) == full, KD, count)
    return (rows, columns, count)


def draw_tile_rows(key, part):
    return tile_layout(key)[0]


def draw_tile_columns(key, part):
    return tile_layout(key)[1]


def draw_tile_count(key, part):
    return tile_layout(key)[2]


def draw_dipole_rows(key, part):
    return dipole_layout(key)[0]


def draw_dipole_columns(key, part):
    return dipole_layout(key)[1]


def draw_dipole_count(key, part):
    return dipole_layout(key)[2]


def levels(own_key, extent, cuts, low, largest):
    gain, own = 1.0, jax.random.fold_in(own_key, 6)
    for position, blocks in cuts:
        steps = jnp.exp(jax.random.uniform(jax.random.fold_in(own, position), (blocks,), jnp.float32, low / len(cuts), largest / len(cuts)))
        gain = gain * jnp.repeat(steps, extent[position] // blocks).reshape([-1 if axis == position else 1 for axis in range(len(extent))])
    return gain


def scatter_about(own_key, dims, scale, reach, cuts=(), kind=jnp.bfloat16):
    factor_of = levels(own_key, dims, cuts, -0.22, 0.18) if cuts else 1.0
    drawn = jax.random.normal(own_key, dims, jnp.float32) * scale * factor_of
    return jnp.minimum(jnp.maximum(drawn, -reach), reach).astype(kind)


def setup_inputs(seed: int = 0) -> dict:
    keys = jax.random.split(jax.random.key(seed), 11)
    sources = scatter_about(keys[0], (NV, STATES), 1.0, 6.0, ((1, 32),))
    dipole_tiles = scatter_about(keys[1], (ROW_BLOCKS * COL_BLOCKS * KD, BLOCK, BLOCK), (BLOCK * KD // 8) ** -0.5, 0.1875, ((0, 32),))
    dipole_rows = draw_dipole_rows(jax.random.fold_in(keys[10], 71), 0)
    dipole_columns = draw_dipole_columns(jax.random.fold_in(keys[10], 71), 0)
    dipole_count = draw_dipole_count(jax.random.fold_in(keys[10], 71), 0)
    energies = jnp.clip(jax.random.uniform(keys[5], (STATES,), jnp.float32, -3.0, 3.0) * levels(keys[5], (STATES,), ((0, 32),), -0.4, 0.0), -3.0, 3.0)
    h_tiles = scatter_about(keys[6], (ROW_BLOCKS * COL_BLOCKS * KT, BLOCK, BLOCK), (BLOCK * KT) ** -0.5, 0.0625, ((0, 32),))
    tile_rows = draw_tile_rows(jax.random.fold_in(keys[10], 71), 0)
    tile_columns = draw_tile_columns(jax.random.fold_in(keys[10], 71), 0)
    tile_count = draw_tile_count(jax.random.fold_in(keys[10], 71), 0)
    return dict(sources=sources, dipole_tiles=dipole_tiles, dipole_rows=dipole_rows, dipole_columns=dipole_columns, dipole_count=dipole_count, energies=energies, h_tiles=h_tiles, tile_rows=tile_rows, tile_columns=tile_columns, tile_count=tile_count)


EPSILON = 1e-06

def split_value(vectors):
    upper = vectors.astype(jnp.bfloat16)
    rest = vectors - lax.optimization_barrier(upper).astype(jnp.float32)
    lower = rest.astype(jnp.bfloat16)
    return upper.astype(jnp.float32) + lax.optimization_barrier(lower).astype(jnp.float32)

def block_apply(vectors, tiles, tile_rows, tile_columns, counts, slots, transposed):
    total_blocks = ROW_BLOCKS * COL_BLOCKS
    height = vectors.shape[0]
    blocks = vectors.reshape(height, total_blocks, BLOCK).transpose(1, 0, 2)
    tiles_dev = tiles.reshape(total_blocks, slots, BLOCK, BLOCK)

    def visit(totals, item):
        device, tile_set, row_set, column_set, live_count = item
        upper_block = device // ROW_BLOCKS * ROW_BLOCKS + row_set
        lower_block = column_set * ROW_BLOCKS + device % ROW_BLOCKS
        live = (jnp.arange(slots, dtype=jnp.int32) < live_count).astype(jnp.float32)
        weights = tile_set.astype(jnp.float32)
        picked = blocks[lower_block]
        direct = jnp.einsum('tvs,tks->tvk', picked, weights, precision=lax.Precision.HIGHEST)
        totals = totals.at[upper_block].add(direct * live[:, None, None])
        if transposed:
            picked = blocks[upper_block]
            back = jnp.einsum('tvk,tks->tvs', picked, weights, precision=lax.Precision.HIGHEST)
            totals = totals.at[lower_block].add(back * live[:, None, None])
        return (totals, None)
    start = jnp.zeros((total_blocks, height, BLOCK), jnp.float32)
    totals, unused = lax.scan(visit, start, (jnp.arange(total_blocks, dtype=jnp.int32), tiles_dev, tile_rows.reshape(total_blocks, slots), tile_columns.reshape(total_blocks, slots), counts))
    return totals.transpose(1, 0, 2).reshape(height, total_blocks * BLOCK)

def reference(sources, dipole_tiles, dipole_rows, dipole_columns, dipole_count, energies, h_tiles, tile_rows, tile_columns, tile_count):
    phi = block_apply(sources.astype(jnp.float32), dipole_tiles, dipole_rows, dipole_columns, dipole_count, KD, False)
    rhs = jnp.tile(phi, (SHIFTS, 1))
    centre = (jnp.arange(SHIFTS * NV, dtype=jnp.int32) // NV).astype(jnp.float32)
    shift = (-2.0 + 4.0 * (centre + 0.5) / SHIFTS)[:, None]

    def hamiltonian(vectors):
        return energies[None, :] * vectors + block_apply(split_value(vectors), h_tiles, tile_rows, tile_columns, tile_count, KT, True)

    def lorentz(vectors):
        inner = hamiltonian(vectors) - shift * vectors
        return hamiltonian(inner) - shift * inner + vectors
    solution = jnp.zeros_like(rhs)
    residual = rhs
    direction = rhs
    norm_now = lax.optimization_barrier(jnp.sum(residual * residual, axis=1))
    checks = []
    for index in range(ITERS):
        image = lorentz(direction)
        curvature = lax.optimization_barrier(jnp.sum(direction * image, axis=1))
        image_sum = lax.optimization_barrier(jnp.sum(image, axis=1))
        image_square = lax.optimization_barrier(jnp.sum(image * image, axis=1))
        checks.append(image_sum / jnp.sqrt(image_square + EPSILON))
        alpha = norm_now / curvature
        solution = solution + alpha[:, None] * direction
        residual = residual - alpha[:, None] * image
        norm_next = lax.optimization_barrier(jnp.sum(residual * residual, axis=1))
        direction = residual + (norm_next / norm_now)[:, None] * direction
        norm_now = norm_next
    return (solution, residual, jnp.stack(checks, axis=0))
```

```python
import jax
import jax.numpy as jnp
from jax import lax
from jax.sharding import PartitionSpec as P

SHIFTS = 4
ITERS = 3
EPSILON = 1e-06


def split_parts(vectors):
    upper = vectors.astype(jnp.bfloat16)
    rest = vectors - lax.optimization_barrier(upper).astype(jnp.float32)
    return jnp.concatenate([upper, rest.astype(jnp.bfloat16)], axis=-2)


def one_hot(index, size, live):
    hits = (index[:, None] == jnp.arange(size, dtype=jnp.int32)[None, :]) & live[:, None]
    return hits.astype(jnp.bfloat16)


def live_slots(slots, count):
    return jnp.arange(slots, dtype=jnp.int32) < count[0]


def expand(out_hits, in_hits, blocks):
    select = out_hits[:, :, None] * in_hits[:, None, :]
    picked = jnp.einsum("tic,cvs->tivs", select, blocks, preferred_element_type=jnp.float32)
    t, i, v, s = picked.shape
    return picked.astype(jnp.bfloat16).reshape(t, i * v, s)


def place(direct, mirror):
    row, col = lax.axis_index("row"), lax.axis_index("col")
    row_groups, column_groups = lax.axis_size("col"), lax.axis_size("row")
    at_row = (jnp.arange(column_groups) == row)[:, None, None, None]
    total = jnp.where(at_row, direct[None], 0.0)
    if mirror is not None:
        at_col = (jnp.arange(row_groups) == col)[None, :, None, None]
        total = total + jnp.where(at_col, mirror[:, None], 0.0)
    return lax.psum(total, ("row", "col"))


def dots(a, b):
    return jnp.sum(a * b, axis=(0, 1, 3))


def body(sources, dipole_tiles, dipole_rows, dipole_columns, dipole_count, energies, h_tiles, tile_rows, tile_columns, tile_count):
    row, col = lax.axis_index("row"), lax.axis_index("col")
    row_groups, column_groups = lax.axis_size("col"), lax.axis_size("row")
    height, width = sources.shape
    slots = h_tiles.shape[0]

    gathered = lax.all_gather(sources, "row", axis=0)
    live = live_slots(dipole_tiles.shape[0], dipole_count)
    lhs = expand(one_hot(dipole_rows, row_groups, live), one_hot(dipole_columns, column_groups, live), gathered)
    field = jnp.einsum("tus,tks->uk", lhs, dipole_tiles, preferred_element_type=jnp.float32)
    phi = place(field.reshape(row_groups, height, width), None)

    live = live_slots(slots, tile_count)
    row_hits = one_hot(tile_rows, row_groups, live)
    col_hits = one_hot(tile_columns, column_groups, live)

    def hamiltonian(b):
        parts = split_parts(b)
        by_col = lax.dynamic_index_in_dim(parts, col, 1, keepdims=False)
        by_row = lax.dynamic_index_in_dim(parts, row, 0, keepdims=False)
        own = lax.dynamic_index_in_dim(lax.dynamic_index_in_dim(b, row, 0, keepdims=False), col, 0, keepdims=False)
        direct = jnp.einsum(
            "tus,tks->uk", expand(row_hits, col_hits, by_col), h_tiles, preferred_element_type=jnp.float32
        ).reshape(row_groups, 2, height, width).sum(axis=1)
        mirror = jnp.einsum(
            "tuk,tks->us", expand(col_hits, row_hits, by_row), h_tiles, preferred_element_type=jnp.float32
        ).reshape(column_groups, 2, height, width).sum(axis=1)
        at = (jnp.arange(row_groups) == col)[:, None, None]
        direct = direct + jnp.where(at, (own * energies[None, :])[None], 0.0)
        return place(direct, mirror)

    steps = 2 * ITERS
    zero = jnp.zeros((height,), jnp.float32)
    basis = [phi]
    gram = [[zero] * (steps + 1) for _ in range(steps + 1)]
    hess = [[zero] * (steps + 1) for _ in range(steps + 1)]
    sums = []
    for j in range(steps):
        w = hamiltonian(basis[j])
        for i in range(j + 1):
            gram[i][j] = gram[j][i] = dots(basis[i], basis[j])
        sums.append(jnp.sum(basis[j], axis=(0, 1, 3)))
        if j + 1 < steps:
            size = dots(w, w)
            left = size
            rest = w
            for i in range(j + 1):
                d = dots(w, basis[i])
                norm = jnp.where(gram[i][i] > 0, gram[i][i], 1.0)
                h = d / norm
                hess[i][j] = h
                left = left - h * d
                rest = rest - h[:, None] * basis[i]
            left = jnp.maximum(left, size * 1e-9)
            scale = jnp.sqrt(jnp.where(left > 0, left, 1.0))
            hess[j + 1][j] = scale
            basis.append(rest / scale[:, None])
        else:
            hess[steps][j] = zero + 1.0
            basis.append(w)
            for i in range(steps + 1):
                gram[i][steps] = gram[steps][i] = dots(basis[i], w)
            sums.append(jnp.sum(w, axis=(0, 1, 3)))

    tile = lambda x: jnp.tile(x, (1,) * (x.ndim - 1) + (SHIFTS,))
    gram = tile(jnp.stack([jnp.stack(line) for line in gram]))
    hess = tile(jnp.stack([jnp.stack(line) for line in hess]))
    sums = tile(jnp.stack(sums))
    centre = (jnp.arange(SHIFTS * height, dtype=jnp.int32) // height).astype(jnp.float32)
    shift = -2.0 + 4.0 * (centre + 0.5) / SHIFTS

    def along(matrix, x):
        return jnp.sum(matrix * x[None], axis=1)

    def inner(x, y):
        return jnp.sum(x * along(gram, y), axis=0)

    first = (jnp.arange(steps + 1) == 0)[:, None]
    residual = jnp.where(first, jnp.ones_like(shift)[None], 0.0)
    direction = residual
    answer = jnp.zeros_like(residual)
    norm_now = inner(residual, residual)
    checks = []
    for index in range(ITERS):
        u = along(hess, direction) - shift * direction
        image = along(hess, u) - shift * u + direction
        curvature = inner(direction, image)
        checks.append(jnp.sum(sums * image, axis=0) / jnp.sqrt(inner(image, image) + EPSILON))
        alpha = norm_now / curvature
        answer = answer + alpha * direction
        residual = residual - alpha * image
        norm_next = inner(residual, residual)
        direction = residual + (norm_next / norm_now) * direction
        norm_now = norm_next

    own = [
        lax.dynamic_index_in_dim(lax.dynamic_index_in_dim(b, row, 0, keepdims=False), col, 0, keepdims=False)
        for b in basis
    ]

    def combine(x):
        x = x.reshape(steps + 1, SHIFTS, height, 1)
        return sum(x[i] * own[i][None] for i in range(steps + 1)).reshape(SHIFTS * height, width)

    return combine(answer), combine(residual), jnp.stack(checks)


def solution(mesh):
    both = ("row", "col")
    return jax.shard_map(
        body,
        mesh=mesh,
        in_specs=(
            P(None, both),
            P(both, None, None),
            P(both),
            P(both),
            P(both),
            P(both),
            P(both, None, None),
            P(both),
            P(both),
            P(both),
        ),
        out_specs=(P(None, both), P(None, both), P()),
        check_vma=False,
    )
```

```python
import functools

import jax
import jax.numpy as jnp
from jax import lax
from jax.experimental import pallas as pl
from jax.experimental.pallas import tpu as pltpu
from jax.sharding import PartitionSpec as P

SHIFTS = 4
ITERS = 3
EPSILON = 1e-06
LANES = 128
STEPS = 2 * ITERS
MESH = pl.DeviceIdType.MESH
SIZE, SUM, GRAM, BASIS_SUM, SLOTS = STEPS, STEPS + 1, STEPS + 2, 2 * STEPS + 2, 16
SOURCES, FIELD, VECTORS, TERMS, DOTS, LOADS = 0, 1, 2, STEPS + 2, 2 * STEPS + 2, 3 * STEPS + 2


def kernel(
    columns,
    rows,
    sources,
    energies,
    d_tiles,
    h_tiles,
    d_columns,
    d_mask,
    h_slot,
    h_live,
    answer_ref,
    residual_ref,
    check_ref,
    d_held,
    h_held,
    table,
    source_set,
    field_out,
    field_in,
    col_set,
    row_set,
    col_out,
    row_out,
    col_in,
    row_in,
    col_parts,
    row_parts,
    dot_set,
    raw,
    col_send,
    col_recv,
    row_send,
    row_recv,
    load_sem,
):
    row, col = lax.axis_index("row"), lax.axis_index("col")
    devices = columns * rows
    me = row * rows + col
    height, width = sources.shape
    slots = d_tiles.shape[0]

    load_d = pltpu.make_async_copy(d_tiles, d_held, load_sem.at[0])
    load_h = pltpu.make_async_copy(h_tiles, h_held, load_sem.at[1])
    load_d.start()
    load_h.start()

    def peer(k):
        other = lax.rem(me + k, devices)
        return (lax.div(other, rows), lax.rem(other, rows))

    barrier = pltpu.get_barrier_semaphore()

    @pl.loop(1, devices)
    def _(k):
        pl.semaphore_signal(barrier, inc=1, device_id=peer(k), device_id_type=MESH)

    pl.semaphore_wait(barrier, devices - 1)

    def to_col_set(src, dst, phase, k):
        to = lax.rem(row + k, columns)
        pltpu.make_async_remote_copy(
            src_ref=src(to),
            dst_ref=dst,
            send_sem=col_send.at[phase],
            recv_sem=col_recv.at[phase],
            device_id=(to, col),
            device_id_type=MESH,
        ).start()

    def to_row_set(src, dst, phase, k):
        to = lax.rem(col + k, rows)
        pltpu.make_async_remote_copy(
            src_ref=src(to),
            dst_ref=dst,
            send_sem=row_send.at[phase],
            recv_sem=row_recv.at[phase],
            device_id=(row, to),
            device_id_type=MESH,
        ).start()

    def wait_for(ref, count, sem):
        part = ref.at[pl.ds(0, count)]
        pltpu.make_async_copy(part, part, sem).wait()

    source_set[row] = sources[...]
    for k in range(1, columns):
        to_col_set(lambda to: source_set.at[row], source_set.at[row], SOURCES, k)
    load_d.wait()
    wait_for(source_set, columns - 1, col_recv.at[SOURCES])

    def slot_term(t, total):
        picked = source_set[d_columns[t]].astype(jnp.float32)
        lhs = jnp.concatenate([picked * d_mask[i * slots + t] for i in range(rows)], axis=0)
        return total + lax.dot_general(
            lhs.astype(jnp.bfloat16), d_held[t], (((1,), (1,)), ((), ())), preferred_element_type=jnp.float32
        )

    total = lax.fori_loop(0, slots, slot_term, jnp.zeros((rows * height, width), jnp.float32))
    for i in range(rows):
        field_out[i] = total[i * height : (i + 1) * height]
    for k in range(1, rows):
        to_row_set(lambda to: field_out.at[to], field_in.at[col], FIELD, k)
    field_in[col] = field_out[col]

    load_h.wait()

    @pl.loop(0, columns)
    def _(c):
        for i in range(rows):
            at = i * columns + c
            tile = h_held[h_slot[at]]
            table[c, i * width : (i + 1) * width, :] = jnp.where(h_live[at] > 0, tile, jnp.zeros_like(tile))

    wait_for(field_in, rows - 1, row_recv.at[FIELD])
    phi = field_in[0]
    for i in range(1, rows):
        phi = phi + field_in[i]

    lane = lax.broadcasted_iota(jnp.int32, (height, LANES), 1)
    sub = lax.broadcasted_iota(jnp.int32, (height, LANES), 0)
    per_row = LANES // height
    dot_lane = lax.broadcasted_iota(jnp.int32, (SLOTS, LANES), 1)
    dot_sub = lax.broadcasted_iota(jnp.int32, (SLOTS, LANES), 0)
    dot_rows = SLOTS // per_row

    def gather(step, vector):
        raw[step] = vector
        col_set[step, row] = vector
        row_set[step, col] = vector
        for k in range(1, columns):
            to_col_set(lambda to: raw.at[step], col_set.at[step, row], VECTORS + step, k)
        for k in range(1, rows):
            to_row_set(lambda to: raw.at[step], row_set.at[step, col], VECTORS + step, k)

    def gathered(step):
        wait_for(col_set.at[step], columns - 1, col_recv.at[VECTORS + step])
        wait_for(row_set.at[step], rows - 1, row_recv.at[VECTORS + step])

    def split(step):
        @pl.loop(0, columns)
        def _(c):
            b = col_set[step, c]
            upper = b.astype(jnp.bfloat16)
            col_parts[c] = jnp.concatenate([upper, (b - upper.astype(jnp.float32)).astype(jnp.bfloat16)], axis=0)

        for i in range(rows):
            b = row_set[step, i]
            upper = b.astype(jnp.bfloat16)
            row_parts[:, i * width : (i + 1) * width] = jnp.concatenate(
                [upper, (b - upper.astype(jnp.float32)).astype(jnp.bfloat16)], axis=0
            )

    def hamiltonian(step):
        phase = TERMS + step

        def column(k, total):
            c = lax.rem(row + k, columns)
            m = jnp.dot(row_parts[...], table[c], preferred_element_type=jnp.float32)
            col_out[step, c] = m[:height] + m[height:]

            @pl.when(k < columns)
            def _():
                to_col_set(lambda to: col_out.at[step, to], col_in.at[step, row], phase, k)

            return total + lax.dot_general(
                col_parts[c], table[c], (((1,), (1,)), ((), ())), preferred_element_type=jnp.float32
            )

        total = lax.fori_loop(1, columns + 1, column, jnp.zeros((2 * height, rows * width), jnp.float32))
        total = total[:height] + total[height:]
        for i in range(rows):
            row_out[step, i] = total[:, i * width : (i + 1) * width]
        for k in range(1, rows):
            to_row_set(lambda to: row_out.at[step, to], row_in.at[step, col], phase, k)
        col_in[step, row] = col_out[step, row]
        row_in[step, col] = row_out[step, col]
        w = energies[...] * col_set[step, row]
        wait_for(col_in.at[step], columns - 1, col_recv.at[phase])
        wait_for(row_in.at[step], rows - 1, row_recv.at[phase])
        for c in range(columns):
            w = w + col_in[step, c]
        for i in range(rows):
            w = w + row_in[step, i]
        return w

    def send_dots(step, w):
        def column(x):
            return jnp.sum(x, axis=1, keepdims=True)

        now = col_set[step, row]
        cells = {SIZE: column(w * w), SUM: column(w), BASIS_SUM: column(now)}
        for i in range(step + 1):
            b = col_set[i, row]
            cells[i] = column(w * b)
            cells[GRAM + i] = column(now * b)
        packed = [jnp.zeros((height, LANES), jnp.float32) for _ in range(dot_rows)]
        for d, cell in cells.items():
            at = d // per_row
            packed[at] = packed[at] + jnp.where(lane == d % per_row * height + sub, cell, 0.0)
        for at in range(dot_rows):
            dot_set[step, me, at : at + 1, :] = jnp.sum(packed[at], axis=0, keepdims=True)

        @pl.loop(1, devices)
        def _(k):
            pltpu.make_async_remote_copy(
                src_ref=dot_set.at[step, me],
                dst_ref=dot_set.at[step, me],
                send_sem=col_send.at[DOTS + step],
                recv_sem=col_recv.at[DOTS + step],
                device_id=peer(k),
                device_id_type=MESH,
            ).start()

    def read_dots(step):
        wait_for(dot_set.at[step], devices - 1, col_recv.at[DOTS + step])
        total = jnp.sum(dot_set[step], axis=0)
        spread = jnp.concatenate(
            [jnp.broadcast_to(total[at : at + 1], (per_row, LANES)) for at in range(dot_rows)], axis=0
        )
        spread = jnp.where(dot_lane // height == dot_sub % per_row, spread, 0.0)
        turn = height
        while turn < LANES:
            spread = spread + pltpu.roll(spread, turn, 1)
            turn *= 2
        return [spread[d : d + 1] for d in range(SLOTS)]

    def as_column(line):
        return jnp.sum(jnp.where(lane == sub, line, 0.0), axis=1, keepdims=True)

    zero = jnp.zeros((1, LANES), jnp.float32)
    one = zero + 1.0
    size = STEPS + 1
    gram = [[None] * size for _ in range(size)]
    hess = [[None] * size for _ in range(size)]
    sums = []

    gather(0, phi)
    gathered(0)
    split(0)
    for step in range(STEPS):
        w = hamiltonian(step)
        if step + 1 < STEPS:
            gather(step + 1, w)
        else:
            raw[STEPS] = w
        send_dots(step, w)
        found = read_dots(step)
        sums.append(found[BASIS_SUM])
        for i in range(step + 1):
            gram[i][step] = gram[step][i] = found[GRAM + i]
        if step + 1 == STEPS:
            hess[STEPS][step] = one
            for i in range(step + 1):
                gram[i][STEPS] = gram[STEPS][i] = found[i]
            gram[STEPS][STEPS] = found[SIZE]
            sums.append(found[SUM])
            break
        left = found[SIZE]
        for i in range(step + 1):
            norm = jnp.where(gram[i][i] > 0, gram[i][i], 1.0)
            hess[i][step] = found[i] / norm
            left = left - hess[i][step] * found[i]
        left = jnp.maximum(left, found[SIZE] * 1e-9)
        left = jnp.where(left > 0, left, 1.0)
        scale = jnp.sqrt(left)
        hess[step + 1][step] = scale
        inverse = 1.0 / scale
        shares = [as_column(hess[i][step] * inverse) for i in range(step + 1)]
        inverse = as_column(inverse)
        gathered(step + 1)
        for blocks, count in ((col_set, columns), (row_set, rows)):

            @pl.loop(0, count)
            def _(c, blocks=blocks):
                b = blocks[step + 1, c] * inverse
                for i in range(step + 1):
                    b = b - shares[i] * blocks[i, c]
                blocks[step + 1, c] = b

        split(step + 1)

    centre = (lax.broadcasted_iota(jnp.int32, (1, LANES), 1) // height).astype(jnp.float32)
    shift = -2.0 + 4.0 * (centre + 0.5) / SHIFTS

    def plus(terms):
        terms = [t for t in terms if t is not None]
        return functools.reduce(lambda a, b: a + b, terms) if terms else None

    def times(a, b):
        return None if a is None or b is None else a * b

    def minus(a, b):
        return a if b is None else (-b if a is None else a - b)

    def apply(x):
        return [
            minus(plus([times(hess[i][j], x[j]) for j in range(size)]), times(shift, x[i])) for i in range(size)
        ]

    def inner(x, y):
        return plus([times(x[i], plus([times(gram[i][j], y[j]) for j in range(size)])) for i in range(size)])

    residual = [one] + [None] * STEPS
    direction = residual
    answer = [None] * size
    norm_now = inner(residual, residual)
    for index in range(ITERS):
        image = [plus([a, d]) for a, d in zip(apply(apply(direction)), direction)]
        total = plus([times(sums[i], image[i]) for i in range(size)])
        check = total / jnp.sqrt(inner(image, image) + EPSILON)
        check_ref[index : index + 1, :] = check[:, : SHIFTS * height]
        alpha = norm_now / inner(direction, image)
        answer = [plus([x, times(alpha, d)]) for x, d in zip(answer, direction)]
        residual = [minus(r, times(alpha, a)) for r, a in zip(residual, image)]
        if index + 1 < ITERS:
            norm_next = inner(residual, residual)
            direction = [plus([r, times(norm_next / norm_now, d)]) for r, d in zip(residual, direction)]
            norm_now = norm_next

    for out, x in ((answer_ref, answer), (residual_ref, residual)):
        for k in range(SHIFTS):
            value = None
            for i in range(size):
                if x[i] is not None:
                    share = jnp.sum(jnp.where(lane == k * height + sub, x[i], 0.0), axis=1, keepdims=True)
                    value = plus([value, share * (col_set[i, row] if i < STEPS else raw[STEPS])])
            out[k * height : (k + 1) * height, :] = value

    wait_for(source_set, columns - 1, col_send.at[SOURCES])
    wait_for(field_out, rows - 1, row_send.at[FIELD])
    for step in range(STEPS):
        wait_for(col_set.at[step], columns - 1, col_send.at[VECTORS + step])
        wait_for(row_set.at[step], rows - 1, row_send.at[VECTORS + step])
        wait_for(col_out.at[step], columns - 1, col_send.at[TERMS + step])
        wait_for(row_out.at[step], rows - 1, row_send.at[TERMS + step])
        wait_for(dot_set.at[step], devices - 1, col_send.at[DOTS + step])


def body(sources, d_tiles, d_rows, d_columns, d_count, energies, h_tiles, h_rows, h_columns, h_count):
    columns, rows = lax.axis_size("row"), lax.axis_size("col")
    height, width = sources.shape
    slots = h_tiles.shape[0]
    d_slots = d_tiles.shape[0]
    index = jnp.arange(d_slots, dtype=jnp.int32)
    hits = (d_rows[None, :] == jnp.arange(rows, dtype=jnp.int32)[:, None]) & (index < d_count[0])[None, :]
    d_mask = hits.astype(jnp.float32).reshape(-1)
    index = jnp.arange(slots, dtype=jnp.int32)
    place = jnp.arange(rows * columns, dtype=jnp.int32)
    hits = ((h_rows * columns + h_columns)[None, :] == place[:, None]) & (index < h_count[0])[None, :]
    h_live = jnp.sum(hits.astype(jnp.int32), axis=1)
    h_slot = jnp.sum(jnp.where(hits, index[None, :], 0), axis=1)

    f32, bf16 = jnp.float32, jnp.bfloat16
    vmem, smem, anywhere = (pl.BlockSpec(memory_space=m) for m in (pltpu.VMEM, pltpu.SMEM, pl.ANY))
    block = (height, width)
    phases = 3 * STEPS + 2
    return pl.pallas_call(
        functools.partial(kernel, columns, rows),
        out_shape=(
            jax.ShapeDtypeStruct((SHIFTS * height, width), f32),
            jax.ShapeDtypeStruct((SHIFTS * height, width), f32),
            jax.ShapeDtypeStruct((ITERS, SHIFTS * height), f32),
        ),
        in_specs=[vmem, vmem, anywhere, anywhere, smem, smem, smem, smem],
        out_specs=(vmem, vmem, vmem),
        scratch_shapes=[
            pltpu.VMEM(d_tiles.shape, bf16),
            pltpu.VMEM(h_tiles.shape, bf16),
            pltpu.VMEM((columns, rows * width, width), bf16),
            pltpu.VMEM((columns, *block), bf16),
            pltpu.VMEM((rows, *block), f32),
            pltpu.VMEM((rows, *block), f32),
            pltpu.VMEM((STEPS, columns, *block), f32),
            pltpu.VMEM((STEPS, rows, *block), f32),
            pltpu.VMEM((STEPS, columns, *block), f32),
            pltpu.VMEM((STEPS, rows, *block), f32),
            pltpu.VMEM((STEPS, columns, *block), f32),
            pltpu.VMEM((STEPS, rows, *block), f32),
            pltpu.VMEM((columns, 2 * height, width), bf16),
            pltpu.VMEM((2 * height, rows * width), bf16),
            pltpu.VMEM((STEPS, rows * columns, SLOTS * height // LANES, LANES), f32),
            pltpu.VMEM((STEPS + 1, *block), f32),
            pltpu.SemaphoreType.DMA((phases,)),
            pltpu.SemaphoreType.DMA((phases,)),
            pltpu.SemaphoreType.DMA((phases,)),
            pltpu.SemaphoreType.DMA((phases,)),
            pltpu.SemaphoreType.DMA((2,)),
        ],
        compiler_params=pltpu.CompilerParams(
            collective_id=0, has_side_effects=True, vmem_limit_bytes=56 * 2**20
        ),
    )(sources, energies[None, :], d_tiles, h_tiles, d_columns, d_mask, h_slot, h_live)


def solution(mesh):
    both = ("row", "col")
    return jax.shard_map(
        body,
        mesh=mesh,
        in_specs=(
            P(None, both),
            P(both, None, None),
            P(both),
            P(both),
            P(both),
            P(both),
            P(both, None, None),
            P(both),
            P(both),
            P(both),
        ),
        out_specs=(P(None, both), P(None, both), P()),
        check_vma=False,
    )
```

```python
import functools

import jax
import jax.numpy as jnp
from jax import lax
from jax.experimental import pallas as pl
from jax.experimental.pallas import tpu as pltpu
from jax.sharding import PartitionSpec as P

SHIFTS = 4
ITERS = 3
EPSILON = 1e-06
LANES = 128
STEPS = 2 * ITERS
MESH = pl.DeviceIdType.MESH
SIZE, SUM, GRAM, BASIS_SUM, SLOTS = STEPS, STEPS + 1, STEPS + 2, 2 * STEPS + 2, 16
SOURCES, FIELD, VECTORS, TERMS, DOTS, LOADS = 0, 1, 2, STEPS + 2, 2 * STEPS + 2, 3 * STEPS + 2


def kernel(
    columns,
    rows,
    sources,
    energies,
    d_tiles,
    h_tiles,
    d_columns,
    d_rows,
    d_count,
    h_slot,
    basis_ref,
    gram_ref,
    hess_ref,
    sums_ref,
    d_held,
    h_held,
    table,
    source_set,
    field_out,
    field_in,
    col_set,
    row_set,
    col_out,
    row_out,
    col_in,
    row_in,
    col_parts,
    row_parts,
    dot_set,
    raw,
    col_send,
    col_recv,
    row_send,
    row_recv,
    load_sem,
):
    row, col = lax.axis_index("row"), lax.axis_index("col")
    devices = columns * rows
    me = row * rows + col
    height, width = sources.shape
    slots = d_tiles.shape[0]

    load_d = pltpu.make_async_copy(d_tiles, d_held, load_sem.at[0])
    load_h = pltpu.make_async_copy(h_tiles, h_held, load_sem.at[1])
    load_d.start()
    load_h.start()

    def peer(k):
        other = lax.rem(me + k, devices)
        return (lax.div(other, rows), lax.rem(other, rows))

    barrier = pltpu.get_barrier_semaphore()

    @pl.loop(1, devices)
    def _(k):
        pl.semaphore_signal(barrier, inc=1, device_id=peer(k), device_id_type=MESH)

    pl.semaphore_wait(barrier, devices - 1)

    def to_col_set(src, dst, phase, k):
        to = lax.rem(row + k, columns)
        pltpu.make_async_remote_copy(
            src_ref=src(to),
            dst_ref=dst,
            send_sem=col_send.at[phase],
            recv_sem=col_recv.at[phase],
            device_id=(to, col),
            device_id_type=MESH,
        ).start()

    def to_row_set(src, dst, phase, k):
        to = lax.rem(col + k, rows)
        pltpu.make_async_remote_copy(
            src_ref=src(to),
            dst_ref=dst,
            send_sem=row_send.at[phase],
            recv_sem=row_recv.at[phase],
            device_id=(row, to),
            device_id_type=MESH,
        ).start()

    def wait_for(ref, count, sem):
        part = ref.at[pl.ds(0, count)]
        pltpu.make_async_copy(part, part, sem).wait()

    source_set[row] = sources[...]
    for k in range(1, columns):
        to_col_set(lambda to: source_set.at[row], source_set.at[row], SOURCES, k)
    load_d.wait()
    wait_for(source_set, columns - 1, col_recv.at[SOURCES])

    def slot_term(t, total):
        picked = source_set[d_columns[t]].astype(jnp.float32)
        to = jnp.where(t < d_count[0], d_rows[t], rows)
        lhs = jnp.concatenate([jnp.where(to == i, picked, 0.0) for i in range(rows)], axis=0)
        return total + lax.dot_general(
            lhs.astype(jnp.bfloat16), d_held[t], (((1,), (1,)), ((), ())), preferred_element_type=jnp.float32
        )

    total = lax.fori_loop(0, slots, slot_term, jnp.zeros((rows * height, width), jnp.float32), unroll=8)
    for i in range(rows):
        field_out[i] = total[i * height : (i + 1) * height]
    for k in range(1, rows):
        to_row_set(lambda to: field_out.at[to], field_in.at[col], FIELD, k)
    field_in[col] = field_out[col]

    load_h.wait()

    @pl.loop(0, columns)
    def _(c):
        for i in range(rows):
            at = i * columns + c
            slot = h_slot[at]
            tile = h_held[jnp.maximum(slot - 1, 0)]
            table[c, i * width : (i + 1) * width, :] = jnp.where(slot > 0, tile, jnp.zeros_like(tile))

    wait_for(field_in, rows - 1, row_recv.at[FIELD])
    phi = field_in[0]
    for i in range(1, rows):
        phi = phi + field_in[i]

    lane = lax.broadcasted_iota(jnp.int32, (height, LANES), 1)
    sub = lax.broadcasted_iota(jnp.int32, (height, LANES), 0)
    per_row = LANES // height
    dot_lane = lax.broadcasted_iota(jnp.int32, (SLOTS, LANES), 1)
    dot_sub = lax.broadcasted_iota(jnp.int32, (SLOTS, LANES), 0)
    dot_rows = SLOTS // per_row

    def gather(step, vector):
        raw[step] = vector
        col_set[step, row] = vector
        row_set[step, col] = vector
        for k in range(1, columns):
            to_col_set(lambda to: raw.at[step], col_set.at[step, row], VECTORS + step, k)
        for k in range(1, rows):
            to_row_set(lambda to: raw.at[step], row_set.at[step, col], VECTORS + step, k)

    def gathered(step):
        wait_for(col_set.at[step], columns - 1, col_recv.at[VECTORS + step])
        wait_for(row_set.at[step], rows - 1, row_recv.at[VECTORS + step])

    def split(step):
        @pl.loop(0, columns)
        def _(c):
            b = col_set[step, c]
            upper = b.astype(jnp.bfloat16)
            col_parts[c] = jnp.concatenate([upper, (b - upper.astype(jnp.float32)).astype(jnp.bfloat16)], axis=0)

        for i in range(rows):
            b = row_set[step, i]
            upper = b.astype(jnp.bfloat16)
            row_parts[:, i * width : (i + 1) * width] = jnp.concatenate(
                [upper, (b - upper.astype(jnp.float32)).astype(jnp.bfloat16)], axis=0
            )

    def total_of(x):
        return jnp.sum(x, axis=1, keepdims=True)

    def early_dots(step):
        now = col_set[step, row]
        cells = {GRAM + i: total_of(now * col_set[i, row]) for i in range(step + 1)}
        cells[BASIS_SUM] = total_of(now)
        return cells

    def hamiltonian(step):
        phase = TERMS + step

        def mirror(k):
            c = lax.rem(row + k, columns)
            m = jnp.dot(row_parts[...], table[c], preferred_element_type=jnp.float32)
            m = m[:height] + m[height:]
            if k < columns:
                col_out[step, c] = m
                to_col_set(lambda to: col_out.at[step, to], col_in.at[step, row], phase, k)
            else:
                col_in[step, row] = m

        def direct(k):
            i = lax.rem(col + k, rows)
            at = pl.ds(pl.multiple_of(i * width, width), width)
            m = jnp.zeros((2 * height, width), jnp.float32)
            for c in range(columns):
                m = m + lax.dot_general(
                    col_parts[c], table[c, at, :], (((1,), (1,)), ((), ())), preferred_element_type=jnp.float32
                )
            m = m[:height] + m[height:]
            if k < rows:
                row_out[step, i] = m
                to_row_set(lambda to: row_out.at[step, to], row_in.at[step, col], phase, k)
            else:
                row_in[step, col] = m

        sent = 1
        for k in range(1, rows):
            direct(k)
            until = 1 + (columns - 1) * k // (rows - 1)
            for n in range(sent, until):
                mirror(n)
            sent = until
        direct(rows)
        mirror(columns)
        before = early_dots(step)
        w = energies[...] * col_set[step, row]
        wait_for(col_in.at[step], columns - 1, col_recv.at[phase])
        wait_for(row_in.at[step], rows - 1, row_recv.at[phase])
        for c in range(columns):
            w = w + col_in[step, c]
        for i in range(rows):
            w = w + row_in[step, i]
        return w, before

    def send_dots(step, w, cells):
        cells = dict(cells)
        cells[SIZE], cells[SUM] = total_of(w * w), total_of(w)
        for i in range(step + 1):
            cells[i] = total_of(w * col_set[i, row])
        packed = [jnp.zeros((height, LANES), jnp.float32) for _ in range(dot_rows)]
        for d, cell in cells.items():
            at = d // per_row
            packed[at] = packed[at] + jnp.where(lane == d % per_row * height + sub, cell, 0.0)
        for at in range(dot_rows):
            dot_set[step, me, at : at + 1, :] = jnp.sum(packed[at], axis=0, keepdims=True)

        def to(r, c):
            pltpu.make_async_remote_copy(
                src_ref=dot_set.at[step, me],
                dst_ref=dot_set.at[step, me],
                send_sem=col_send.at[DOTS + step],
                recv_sem=col_recv.at[DOTS + step],
                device_id=(r, c),
                device_id_type=MESH,
            ).start()

        others = [lax.rem(col + k, rows) for k in range(rows)]
        for c in others[1:]:
            to(row, c)

        @pl.loop(1, columns)
        def _(k):
            r = lax.rem(row + k, columns)
            for c in others:
                to(r, c)

    def read_dots(step):
        wait_for(dot_set.at[step], devices - 1, col_recv.at[DOTS + step])
        total = jnp.sum(dot_set[step], axis=0)
        spread = jnp.concatenate(
            [jnp.broadcast_to(total[at : at + 1], (per_row, LANES)) for at in range(dot_rows)], axis=0
        )
        spread = jnp.where(dot_lane // height == dot_sub % per_row, spread, 0.0)
        turn = height
        while turn < LANES:
            spread = spread + pltpu.roll(spread, turn, 1)
            turn *= 2
        return [spread[d : d + 1] for d in range(SLOTS)]

    def as_column(line):
        return jnp.sum(jnp.where(lane == sub, line, 0.0), axis=1, keepdims=True)

    zero = jnp.zeros((1, LANES), jnp.float32)
    one = zero + 1.0
    size = STEPS + 1
    gram = [[None] * size for _ in range(size)]
    hess = [[None] * size for _ in range(size)]
    sums = []

    gather(0, phi)
    gathered(0)
    split(0)
    for step in range(STEPS):
        w, cells = hamiltonian(step)
        if step + 1 < STEPS:
            gather(step + 1, w)
        else:
            raw[STEPS] = w
        send_dots(step, w, cells)
        found = read_dots(step)
        sums.append(found[BASIS_SUM])
        for i in range(step + 1):
            gram[i][step] = gram[step][i] = found[GRAM + i]
        if step + 1 == STEPS:
            hess[STEPS][step] = one
            for i in range(step + 1):
                gram[i][STEPS] = gram[STEPS][i] = found[i]
            gram[STEPS][STEPS] = found[SIZE]
            sums.append(found[SUM])
            break
        left = found[SIZE]
        for i in range(step + 1):
            norm = jnp.where(gram[i][i] > 0, gram[i][i], 1.0)
            hess[i][step] = found[i] / norm
            left = left - hess[i][step] * found[i]
        left = jnp.maximum(left, found[SIZE] * 1e-9)
        left = jnp.where(left > 0, left, 1.0)
        scale = jnp.sqrt(left)
        hess[step + 1][step] = scale
        inverse = 1.0 / scale
        shares = [as_column(hess[i][step] * inverse) for i in range(step + 1)]
        inverse = as_column(inverse)
        gathered(step + 1)
        for blocks, count in ((col_set, columns), (row_set, rows)):

            @pl.loop(0, count)
            def _(c, blocks=blocks):
                b = blocks[step + 1, c] * inverse
                for i in range(step + 1):
                    b = b - shares[i] * blocks[i, c]
                blocks[step + 1, c] = b

        split(step + 1)

    for step in range(STEPS):
        basis_ref[step] = col_set[step, row]
    basis_ref[STEPS] = raw[STEPS]
    for i in range(size):
        sums_ref[i : i + 1, :] = sums[i]
        for j in range(size):
            gram_ref[i, j : j + 1, :] = gram[i][j]
            hess_ref[i, j : j + 1, :] = zero if hess[i][j] is None else hess[i][j]

    wait_for(source_set, columns - 1, col_send.at[SOURCES])
    wait_for(field_out, rows - 1, row_send.at[FIELD])
    for step in range(STEPS):
        wait_for(col_set.at[step], columns - 1, col_send.at[VECTORS + step])
        wait_for(row_set.at[step], rows - 1, row_send.at[VECTORS + step])
        wait_for(col_out.at[step], columns - 1, col_send.at[TERMS + step])
        wait_for(row_out.at[step], rows - 1, row_send.at[TERMS + step])
        wait_for(dot_set.at[step], devices - 1, col_send.at[DOTS + step])


def finish(basis, gram_ref, hess_ref, sums_ref, answer_ref, residual_ref, check_ref):
    size, height, _ = basis.shape
    lane = lax.broadcasted_iota(jnp.int32, (height, LANES), 1)
    sub = lax.broadcasted_iota(jnp.int32, (height, LANES), 0)
    one = jnp.ones((1, LANES), jnp.float32)
    gram = [[gram_ref[i, j : j + 1, :] for j in range(size)] for i in range(size)]
    hess = [[hess_ref[i, j : j + 1, :] if i <= j + 1 and j < STEPS else None for j in range(size)] for i in range(size)]
    sums = [sums_ref[i : i + 1, :] for i in range(size)]

    centre = (lax.broadcasted_iota(jnp.int32, (1, LANES), 1) // height).astype(jnp.float32)
    shift = -2.0 + 4.0 * (centre + 0.5) / SHIFTS

    def plus(terms):
        terms = [t for t in terms if t is not None]
        return functools.reduce(lambda a, b: a + b, terms) if terms else None

    def times(a, b):
        return None if a is None or b is None else a * b

    def minus(a, b):
        return a if b is None else (-b if a is None else a - b)

    def apply(x):
        return [
            minus(plus([times(hess[i][j], x[j]) for j in range(size)]), times(shift, x[i])) for i in range(size)
        ]

    def inner(x, y):
        return plus([times(x[i], plus([times(gram[i][j], y[j]) for j in range(size)])) for i in range(size)])

    residual = [one] + [None] * STEPS
    direction = residual
    answer = [None] * size
    norm_now = inner(residual, residual)
    for index in range(ITERS):
        image = [plus([a, d]) for a, d in zip(apply(apply(direction)), direction)]
        total = plus([times(sums[i], image[i]) for i in range(size)])
        check = total / jnp.sqrt(inner(image, image) + EPSILON)
        check_ref[index : index + 1, :] = check[:, : SHIFTS * height]
        alpha = norm_now / inner(direction, image)
        answer = [plus([x, times(alpha, d)]) for x, d in zip(answer, direction)]
        residual = [minus(r, times(alpha, a)) for r, a in zip(residual, image)]
        if index + 1 < ITERS:
            norm_next = inner(residual, residual)
            direction = [plus([r, times(norm_next / norm_now, d)]) for r, d in zip(residual, direction)]
            norm_now = norm_next

    for out, x in ((answer_ref, answer), (residual_ref, residual)):
        for k in range(SHIFTS):
            value = None
            for i in range(size):
                if x[i] is not None:
                    share = jnp.sum(jnp.where(lane == k * height + sub, x[i], 0.0), axis=1, keepdims=True)
                    value = plus([value, share * basis[i]])
            out[k * height : (k + 1) * height, :] = value


def body(sources, d_tiles, d_rows, d_columns, d_count, energies, h_tiles, h_rows, h_columns, h_count):
    columns, rows = lax.axis_size("row"), lax.axis_size("col")
    height, width = sources.shape
    slots = h_tiles.shape[0]
    index = jnp.arange(slots, dtype=jnp.int32)
    place = jnp.arange(rows * columns, dtype=jnp.int32)
    hits = ((h_rows * columns + h_columns)[None, :] == place[:, None]) & (index < h_count[0])[None, :]
    h_slot = jnp.sum(jnp.where(hits, index[None, :] + 1, 0), axis=1)

    f32, bf16 = jnp.float32, jnp.bfloat16
    vmem, smem, anywhere = (pl.BlockSpec(memory_space=m) for m in (pltpu.VMEM, pltpu.SMEM, pl.ANY))
    block = (height, width)
    phases = 3 * STEPS + 2
    size = STEPS + 1
    found = pl.pallas_call(
        functools.partial(kernel, columns, rows),
        out_shape=(
            jax.ShapeDtypeStruct((size, *block), f32),
            jax.ShapeDtypeStruct((size, size, LANES), f32),
            jax.ShapeDtypeStruct((size, size, LANES), f32),
            jax.ShapeDtypeStruct((size, LANES), f32),
        ),
        in_specs=[vmem, vmem, anywhere, anywhere, smem, smem, smem, smem],
        out_specs=(vmem,) * 4,
        scratch_shapes=[
            pltpu.VMEM(d_tiles.shape, bf16),
            pltpu.VMEM(h_tiles.shape, bf16),
            pltpu.VMEM((columns, rows * width, width), bf16),
            pltpu.VMEM((columns, *block), bf16),
            pltpu.VMEM((rows, *block), f32),
            pltpu.VMEM((rows, *block), f32),
            pltpu.VMEM((STEPS, columns, *block), f32),
            pltpu.VMEM((STEPS, rows, *block), f32),
            pltpu.VMEM((STEPS, columns, *block), f32),
            pltpu.VMEM((STEPS, rows, *block), f32),
            pltpu.VMEM((STEPS, columns, *block), f32),
            pltpu.VMEM((STEPS, rows, *block), f32),
            pltpu.VMEM((columns, 2 * height, width), bf16),
            pltpu.VMEM((2 * height, rows * width), bf16),
            pltpu.VMEM((STEPS, rows * columns, SLOTS * height // LANES, LANES), f32),
            pltpu.VMEM((STEPS + 1, *block), f32),
            pltpu.SemaphoreType.DMA((phases,)),
            pltpu.SemaphoreType.DMA((phases,)),
            pltpu.SemaphoreType.DMA((phases,)),
            pltpu.SemaphoreType.DMA((phases,)),
            pltpu.SemaphoreType.DMA((2,)),
        ],
        compiler_params=pltpu.CompilerParams(
            collective_id=0, has_side_effects=True, vmem_limit_bytes=56 * 2**20
        ),
    )(sources, energies[None, :], d_tiles, h_tiles, d_columns, d_rows, d_count, h_slot)
    return pl.pallas_call(
        finish,
        out_shape=(
            jax.ShapeDtypeStruct((SHIFTS * height, width), f32),
            jax.ShapeDtypeStruct((SHIFTS * height, width), f32),
            jax.ShapeDtypeStruct((ITERS, SHIFTS * height), f32),
        ),
        in_specs=[vmem] * 4,
        out_specs=(vmem,) * 3,
    )(*found)


def solution(mesh):
    both = ("row", "col")
    return jax.shard_map(
        body,
        mesh=mesh,
        in_specs=(
            P(None, both),
            P(both, None, None),
            P(both),
            P(both),
            P(both),
            P(both),
            P(both, None, None),
            P(both),
            P(both),
            P(both),
        ),
        out_specs=(P(None, both), P(None, both), P()),
        check_vma=False,
    )
```
